256 devices in a mesh: col: 4 (over y), row: 64 (over x, z, core).
Axes of the slice: x: 4, y: 4, z: 8, core: 2. Of those that a mesh axis runs over, the one named last changes fastest.
Arguments:
- factor_blocks: bfloat16 [320, 17, 512, 512], P('row', None, None, 'col'), may hold values from -0.25 to 0.25
- block_scales: float32 [320, 17], P('row'), may hold values from 0.1 to 0.3
- dep_column: int32 [320, 17], P('row'), may hold values from 0 to 383, as said below
- dep_count: int32 [320], P('row'), may hold values from 1 to 17, as said below
- diag_inverse: bfloat16 [384, 512, 512], P('row', 'col'), may hold values from -0.25 to 0.25
- right_side: float32 [384, 512, 256], P('row', 'col'), may hold values from -6 to 6
Outputs:
- solution: bfloat16 [384, 512, 256], P('row', 'col')
The draws below stay inside these ranges and needn't reach their ends.
Inputs may be any that keep to these rules, and one draw needn't show every extreme that they name: `dep_column`: A live entry (slot below dep_count of its row) names supernode shard * 6 + level with a level below its own row's level and a shard at most 4 away from the row's shard; the live entries of a row are distinct; entries past the count name the row's own shard at level 0 and are unused. `dep_count`: at least one, at most the number of possible supernodes within reach; some supernode uses all 17 slots.
All inputs are finite; a program needn't handle non-finite values.
Results may differ from the reference program's by a relative error of at most 0.0054.
Values may be sent and summed in bfloat16 or wider, within the bound.
No kernel may reach another device: no remote copies, remote signals or barrier semaphores. Data moves between devices by JAX's collectives and lax.ppermute only.
A program may use at most 128 MiB of HBM per device.

```python
import math
import jax
import jax.numpy as jnp
from jax import lax

BLOCK = 512
NRHS = 256
LEVELS = 6
DEPS = 17
REACH = 4
SUPERS = 384
DEP_ROWS = 320
N_ROW = 64


def dependency_table(key):
    row_total = N_ROW * (LEVELS - 1)
    span_width = 2 * REACH + 1
    cand_total = (LEVELS - 1) * span_width
    row_ids = jnp.arange(row_total, dtype=jnp.int32)
    shard_index = row_ids // (LEVELS - 1)
    level_index = row_ids % (LEVELS - 1) + 1
    cand_index = jnp.arange(cand_total, dtype=jnp.int32)
    cand_level = cand_index // span_width
    cand_offset = cand_index % span_width - REACH
    target = shard_index[:, None] + cand_offset[None, :]
    usable = (cand_level[None, :] < level_index[:, None]) & (target >= 0) & (target < N_ROW)
    previous = cand_level[None, :] == level_index[:, None] - 1
    noise_bits = jax.random.randint(jax.random.fold_in(key, 11), (row_total, cand_total), 0, 2 ** 20)
    ranking = noise_bits * 128 + cand_index[None, :] + jnp.where(previous, 0, 2 ** 27) + jnp.where(usable, 0, 2 ** 28)
    ranked = jnp.argsort(ranking, axis=1)[:, :DEPS].astype(jnp.int32)
    chosen_level = ranked // span_width
    chosen_shard = shard_index[:, None] + ranked % span_width - REACH
    usable_count = jnp.sum(usable.astype(jnp.int32), axis=1)
    cap_live = jnp.minimum(usable_count, DEPS)
    lowest = jnp.maximum(1, cap_live - cap_live // 4)
    live_count = jax.random.randint(jax.random.fold_in(key, 12), (row_total,), lowest, cap_live + 1)
    live_count = live_count.at[N_ROW // 2 * (LEVELS - 1) + LEVELS - 2].set(DEPS)
    slot_index = jnp.arange(DEPS, dtype=jnp.int32)
    live = slot_index[None, :] < live_count[:, None]
    column = jnp.where(live, chosen_shard * LEVELS + chosen_level, shard_index[:, None] * LEVELS)
    return (column.astype(jnp.int32), live_count.astype(jnp.int32))


def draw_dep_column(key, part):
    return dependency_table(key)[0]


def draw_dep_count(key, part):
    return dependency_table(key)[1]


def steps_of(stream_key, extent, shards, least, largest):
    factor_of = 1.0
    for position, shards_of in shards:
        heights = jax.random.uniform(jax.random.fold_in(jax.random.fold_in(stream_key, 6), position), (shards_of,), jnp.float32, least / len(shards), largest / len(shards))
        factor_of = factor_of * jnp.repeat(jnp.exp(heights), extent[position] // shards_of).reshape((-1,) + (1,) * (len(extent) - 1 - position))
    return factor_of


def scatter_about(key, extent, spread, most, cuts=(), held_as=jnp.bfloat16):
    array = jax.random.normal(key, extent, jnp.float32) * spread
    if len(cuts) > 0:
        array = steps_of(key, extent, cuts, -0.22, 0.18) * array
    return jnp.clip(array, min=-most, max=most).astype(held_as)


def setup_inputs(seed: int = 0) -> dict:
    arg_keys = jax.random.split(jax.random.key(seed), 7)
    return {
        "factor_blocks": scatter_about(arg_keys[0], (DEP_ROWS, DEPS, BLOCK, BLOCK), BLOCK ** -0.5, 0.25, ((0, 64), (3, 4))),
        "block_scales": jnp.clip(jnp.exp(math.log(0.3) - 1.0986123 * jax.random.uniform(arg_keys[1], (DEP_ROWS, DEPS), jnp.float32) ** steps_of(arg_keys[1], (DEP_ROWS, DEPS), ((0, 64),), -0.2, 0.2)), 0.1, 0.3),
        "dep_column": draw_dep_column(jax.random.fold_in(arg_keys[6], 71), 0),
        "dep_count": draw_dep_count(jax.random.fold_in(arg_keys[6], 71), 0),
        "diag_inverse": scatter_about(arg_keys[4], (SUPERS, BLOCK, BLOCK), BLOCK ** -0.5, 0.25, ((0, 64), (1, 4))),
        "right_side": scatter_about(arg_keys[5], (SUPERS, BLOCK, NRHS), 1.0, 6.0, ((0, 64), (1, 4)), jnp.float32),
    }


def reference(factor_blocks, block_scales, dep_column, dep_count, diag_inverse, right_side):
    solution = jnp.zeros((N_ROW * LEVELS, BLOCK, NRHS), jnp.bfloat16)
    for level_index in range(LEVELS):
        if level_index == 0:
            dep_sums = jnp.zeros((N_ROW, BLOCK, NRHS), jnp.float32)
        else:
            def one_row(shard_index):
                dep_row = (shard_index * (LEVELS - 1) + level_index - 1).astype(jnp.int32)
                live_count = dep_count[dep_row]

                def add_slot(slot_index, running):
                    column = dep_column[dep_row, slot_index]
                    product = jnp.dot(factor_blocks[dep_row, slot_index], solution[column], preferred_element_type=jnp.float32)
                    product = block_scales[dep_row, slot_index] * product
                    return running + jnp.where(slot_index < live_count, product, jnp.zeros_like(product))

                return lax.fori_loop(0, DEPS, add_slot, jnp.zeros((BLOCK, NRHS), jnp.float32))

            dep_sums = lax.map(one_row, jnp.arange(N_ROW, dtype=jnp.int32))
        super_ids = (jnp.arange(N_ROW, dtype=jnp.int32) * LEVELS + level_index).astype(jnp.int32)
        residual = right_side[super_ids] - dep_sums
        fresh = jnp.einsum("nij,njr->nir", diag_inverse[super_ids].astype(jnp.float32), residual, precision=lax.Precision.HIGHEST)
        solution = solution.at[super_ids].set(fresh.astype(jnp.bfloat16))
    return solution
```

```python
import functools

import jax
import jax.numpy as jnp
from jax import lax
from jax.experimental import pallas as pl
from jax.experimental.pallas import tpu as pltpu
from jax.sharding import PartitionSpec as P

VMEM = pl.BlockSpec(memory_space=pltpu.VMEM)
SMEM = pl.BlockSpec(memory_space=pltpu.SMEM)
MIB = 2**20


def row_moves(count, delta):
    pairs = []
    for target in range(count):
        step = 2 * delta if target % 2 == 0 else -2 * delta
        pairs.append(((target + step) % count, target))
    return pairs


def swap_moves(count):
    return [(source, source ^ 1) for source in range(count)]


def col_moves(cols, rows, flip):
    pairs = []
    for col in range(cols):
        for row in range(rows):
            partner = col ^ 1 if (row % 2) ^ flip == 0 else cols - 1 - col
            pairs.append((col * rows + row, partner * rows + row))
    return pairs


def turn_moves(cols, rows, turn):
    pairs = []
    for col in range(cols):
        for row in range(rows):
            target = (col + (turn if row % 2 == 0 else -turn)) % cols
            pairs.append((col * rows + row, target * rows + row))
    return pairs


def split(value):
    high = value.astype(jnp.bfloat16)
    return high, (value - high.astype(jnp.float32)).astype(jnp.bfloat16)


def product(left, right):
    return jnp.dot(left, right, preferred_element_type=jnp.float32)


def exact_product(left, right):
    high, low = split(right)
    return product(left, high) + product(left, low)


def first_kernel(meta_ref, diag_ref, own_ref, *refs):
    out_ref = refs[-1]
    share = own_ref.shape[0]
    total = jnp.zeros(out_ref.shape, jnp.float32)
    for index, piece_ref in enumerate((own_ref, *refs[:-1])):
        start = pl.multiple_of(meta_ref[1 + index] * share, share)
        total += exact_product(diag_ref[0, :, pl.ds(start, share)], piece_ref[...])
    out_ref[...] = total.astype(out_ref.dtype)


def solve_kernel(level, diag_ref, sum_ref, far_ref, out_ref):
    residual = sum_ref[...] + far_ref[...].astype(jnp.float32)
    out_ref[...] = exact_product(diag_ref[level], residual).astype(out_ref.dtype)


def slots_kernel(level, level_count, newest, whole, *refs):
    meta_ref, column_ref, count_ref, scale_ref, factor_ref = refs[:5]
    sources = 1 if newest else level - 1
    piece_refs = refs[5 : 5 + 3 * sources]
    refs = refs[5 + 3 * sources :]
    if newest:
        right_ref, refs = refs[0], refs[1:]
        if level > 1:
            older_ref, refs = refs[0], refs[1:]
        if whole is not None:
            diag_ref, refs = refs[0], refs[1:]
            own_ref, refs = refs[0], refs[1:]
            send_refs, refs = refs[:3], refs[3:]
            sum_ref, stored_ref, list_ref = refs
        else:
            sum_ref, coarse_ref, stored_ref, list_ref = refs
    else:
        sum_ref, stored_ref, list_ref = refs
    dep_row = level - 1
    own_chip = meta_ref[0] // 2
    core = meta_ref[0] % 2

    def collect(slot, found):
        from_level = column_ref[dep_row, slot] % level_count
        wanted = from_level == level - 1 if newest else from_level < level - 1

        @pl.when(wanted)
        def _():
            list_ref[found] = slot

        return found + wanted.astype(jnp.int32)

    list_ref[0] = 0
    found = lax.fori_loop(0, count_ref[dep_row], collect, 0)
    list_ref[found] = list_ref[0]

    for source in range(sources):
        pair_ref, mine_ref, other_ref = piece_refs[3 * source : 3 * source + 3]
        stored_ref[source, 0:2] = pair_ref[...]
        stored_ref[source, 2:6] = mine_ref[...]
        stored_ref[source, 6:10] = other_ref[...]

    share = factor_ref.shape[3]
    sum_ref[...] = -older_ref[...] if newest and level > 1 else jnp.zeros_like(sum_ref)
    if newest:
        start = pl.multiple_of(meta_ref[1] * share, share)
        sum_ref[pl.ds(start, share), :] += right_ref[level]

    def slot_product(slot):
        column = column_ref[dep_row, slot]
        shard = column // level_count
        away = shard // 2 - own_chip
        forward = jnp.where(core == 0, away, -away)
        start = jnp.where(
            away == 0, 0, jnp.where(forward > 0, 2 * forward, 4 - 2 * forward)
        )
        piece = stored_ref[0 if newest else column % level_count, start + shard % 2]
        return product(factor_ref[dep_row, slot], piece)

    sign = -1.0 if newest else 1.0

    def add_two(index, carry):
        one, two = list_ref[2 * index], list_ref[2 * index + 1]
        scale_one = sign * scale_ref[dep_row, one]
        scale_two = jnp.where(2 * index + 1 < found, sign * scale_ref[dep_row, two], 0.0)
        sum_ref[...] += scale_one * slot_product(one) + scale_two * slot_product(two)
        return carry

    lax.fori_loop(0, (found + 1) // 2, add_two, 0)
    if newest and whole is None:
        coarse_ref[...] = sum_ref[...].astype(coarse_ref.dtype)
    elif newest:
        high, low = split(sum_ref[...])
        for index in range(4):
            start = pl.multiple_of(meta_ref[1 + index] * share, share)
            block = diag_ref[whole, pl.ds(start, share), :]
            part = product(block, high) + product(block, low)
            if index == 0:
                own_ref[...] = part
            else:
                send_refs[index - 1][...] = part.astype(jnp.bfloat16)


def per_device(factor_blocks, block_scales, dep_column, dep_count, diag_inverse, right_side):
    level_count, share, block_rows = diag_inverse.shape
    slots = factor_blocks.shape[1]
    width = right_side.shape[2]
    rows, cols = lax.axis_size("row"), lax.axis_size("col")
    shard = lax.axis_index("row").astype(jnp.int32)
    col = lax.axis_index("col").astype(jnp.int32)
    even = shard % 2 == 0
    turn = jnp.where(even, 1, -1)
    turns = (2, 1, 3)
    targets = [(col + turn * step) % cols for step in turns]
    origins = [(col - turn * step) % cols for step in turns]
    out_meta = jnp.stack([shard, col, *targets])
    in_meta = jnp.stack([shard, col, *origins])
    tables = (dep_column, dep_count, block_scales)
    solved_shape = jax.ShapeDtypeStruct((share, width), jnp.bfloat16)
    wide = jax.ShapeDtypeStruct((block_rows, width), jnp.float32)

    def call(body, out_shape, smem_count, operands, limit, scratch=(), flops=2**27, name=None):
        return pl.pallas_call(
            body,
            out_shape=out_shape,
            in_specs=[SMEM] * smem_count + [VMEM] * (len(operands) - smem_count),
            out_specs=jax.tree.map(lambda _: VMEM, out_shape),
            scratch_shapes=list(scratch),
            cost_estimate=pl.CostEstimate(flops=flops, bytes_accessed=2 * MIB, transcendentals=0),
            compiler_params=pltpu.CompilerParams(vmem_limit_bytes=limit),
            name=name,
        )(*operands)

    def slots_call(level, newest, whole, pieces, extra, out_shape, scratch=()):
        sources = 1 if newest else level - 1
        return call(
            functools.partial(slots_kernel, level, level_count, newest, whole),
            out_shape,
            4,
            (out_meta, *tables, factor_blocks, *pieces, *extra),
            18 * MIB,
            (
                *scratch,
                pltpu.VMEM((sources, 10, share, width), jnp.bfloat16),
                pltpu.SMEM((slots + 1,), jnp.int32),
            ),
            flops=8 * 2 * block_rows * share * width,
            name=("new" if newest else "old") + "_slots",
        )

    def along_col(value, flip):
        return lax.ppermute(value, ("col", "row"), col_moves(cols, rows, flip))

    def around_col(value, step):
        return lax.ppermute(value, ("col", "row"), turn_moves(cols, rows, step))

    def spread(solved):
        other = lax.ppermute(solved, "row", swap_moves(rows))
        pair = jnp.where(even, jnp.stack([solved, other]), jnp.stack([other, solved]))
        far = lax.ppermute(pair, "row", row_moves(rows, 2))
        near = lax.ppermute(pair, "row", row_moves(rows, 1))
        return pair, near, far

    def share_out(pair, near, far):
        mine = jnp.concatenate([near, far], axis=0)
        theirs = lax.ppermute(mine, "row", swap_moves(rows))
        return [pair, mine, theirs]

    gathered = lax.all_gather(diag_inverse[2:], "col", axis=1, tiled=True)
    outputs = []
    pieces = []
    for level in range(level_count):
        if level == 0:
            own = right_side[0]
            arrived = [around_col(own, step) for step in turns]
            solved = call(
                first_kernel,
                solved_shape,
                1,
                (in_meta, diag_inverse, own, *arrived),
                4 * MIB,
                name="first_solve",
            )
        else:
            extra = [right_side]
            if level > 1:
                extra.append(older)
            newest = pieces[level - 1]
            if level == 1:
                coarse_shape = jax.ShapeDtypeStruct((block_rows, width), jnp.bfloat16)
                exact, coarse = slots_call(1, True, None, newest, extra, [wide, coarse_shape])
                total = exact + along_col(coarse, 0).astype(jnp.float32)
                arrived = along_col(total.astype(jnp.bfloat16), 1)
                solved = call(
                    functools.partial(solve_kernel, level),
                    solved_shape,
                    0,
                    (diag_inverse, total, arrived),
                    4 * MIB,
                    name="solve",
                )
            else:
                own_shape = jax.ShapeDtypeStruct((share, width), jnp.float32)
                own, *parts = slots_call(
                    level,
                    True,
                    level - 2,
                    newest,
                    [*extra, gathered],
                    [own_shape] + [solved_shape] * 3,
                    [pltpu.VMEM((block_rows, width), jnp.float32)],
                )
                arrived = [around_col(part, step) for part, step in zip(parts, turns)]
                total = own
                for part in arrived:
                    total = total + part.astype(jnp.float32)
                solved = total.astype(jnp.bfloat16)
        outputs.append(solved)
        if level + 1 < level_count:
            pair, near, far = spread(solved)
            if level > 0:
                older_pieces = [x for trio in pieces for x in trio]
                pair, older_pieces = lax.optimization_barrier((pair, older_pieces))
                older = slots_call(level + 1, False, None, older_pieces, [], wide)
                near, far, older = lax.optimization_barrier((near, far, older))
            pieces.append(share_out(pair, near, far))
    return jnp.stack(outputs, axis=0)


def solution(mesh):
    in_specs = (
        P("row", None, None, "col"),
        P("row", None),
        P("row", None),
        P("row"),
        P("row", "col", None),
        P("row", "col", None),
    )
    return jax.shard_map(
        per_device, mesh=mesh, in_specs=in_specs, out_specs=P("row", "col", None), check_vma=False
    )
```

```python
import functools

import jax
import jax.numpy as jnp
from jax import lax
from jax.experimental import pallas as pl
from jax.experimental.pallas import tpu as pltpu
from jax.sharding import PartitionSpec as P

VMEM = pl.BlockSpec(memory_space=pltpu.VMEM)
SMEM = pl.BlockSpec(memory_space=pltpu.SMEM)
HBM = pl.BlockSpec(memory_space=pltpu.HBM)
MIB = 2**20
GROUP = 2
TABLE_LIMIT = 2 * MIB
SOON_LIMIT = 48 * MIB
LATE_LIMIT = 40 * MIB


def row_moves(count, delta):
    pairs = []
    for target in range(count):
        step = 2 * delta if target % 2 == 0 else -2 * delta
        pairs.append(((target + step) % count, target))
    return pairs


def swap_moves(count):
    return [(source, source ^ 1) for source in range(count)]


def partners(cols, col, odd):
    one, two = (col ^ 1, cols - 1 - col) if odd == 0 else (cols - 1 - col, col ^ 1)
    return one, two, (col + 2) % cols


def col_moves(cols, rows, which):
    return [
        (col * rows + row, partners(cols, col, row % 2)[which] * rows + row)
        for col in range(cols)
        for row in range(rows)
    ]


def split(value):
    high = value.astype(jnp.bfloat16)
    return high, (value - high.astype(jnp.float32)).astype(jnp.bfloat16)


def product(left, right):
    return jnp.dot(left, right, preferred_element_type=jnp.float32)


def exact_product(left, right):
    high, low = split(right)
    return product(left, high) + product(left, low)


def run_copies(copies):
    for copy in copies:
        copy.start()
    for copy in copies:
        copy.wait()


def fill_kernel(source_ref, start, out_ref, sem):
    run_copies([pltpu.make_async_copy(source_ref.at[pl.ds(start, out_ref.shape[0])], out_ref, sem)])


def soon_fill_kernel(factor_ref, out_ref, sems):
    fill_kernel(factor_ref, 0, out_ref, sems.at[0])


def late_fill_kernel(factor_ref, diag_ref, blocks_ref, late_ref, sems):
    late = late_ref.shape[0]
    run_copies(
        [
            pltpu.make_async_copy(
                factor_ref.at[pl.ds(1, blocks_ref.shape[0])], blocks_ref, sems.at[0]
            ),
            pltpu.make_async_copy(
                diag_ref.at[pl.ds(diag_ref.shape[0] - late, late)], late_ref, sems.at[1]
            ),
        ]
    )


def order_kernel(meta_ref, start_ref, first_ref):
    share = first_ref.shape[1]
    for index in range(4):
        start = pl.multiple_of(meta_ref[1 + index] * share, share)
        first_ref[index] = start_ref[:, pl.ds(start, share)]


def table_kernel(level_count, rows, meta_ref, column_ref, count_ref, scale_ref, index_ref, weight_ref):
    own_chip = meta_ref[0] // 2
    core = meta_ref[0] % 2
    turn = 1 - 2 * core
    room = room_of(index_ref)
    inverse = (2**16 + level_count - 1) // level_count
    for at, dep_row in enumerate(rows):

        def put(position, slot, place, scale):
            index_ref[at, position] = slot
            index_ref[at, 3 * room + position] = place
            weight_ref[at, position] = -scale

        def collect(slot, found):
            column = column_ref[dep_row, slot]
            shard = lax.shift_right_logical(column * inverse, 16)
            from_level = column - shard * level_count
            forward = (lax.shift_right_logical(shard, 1) - own_chip) * turn
            parity = lax.bitwise_and(shard, 1)
            older = from_level != dep_row
            kind = jnp.where(older | (forward == 0), 2, jnp.where(forward > 0, 1, 0))
            place = parity + jnp.where(forward == 0, 0, 2 * jnp.abs(forward) - 2)
            start = jnp.where(forward == 0, 2, jnp.where(forward > 0, 4, 8))
            place = jnp.where(older, 10 * from_level + start + place, place)
            before = jnp.where(kind == 2, found[2], jnp.where(kind == 1, found[1], found[0]))
            put(room * kind + before, slot, place, scale_ref[dep_row, slot])
            return tuple(found[k] + (kind == k).astype(jnp.int32) for k in range(3))

        found = lax.fori_loop(0, count_ref[dep_row], collect, (0, 0, 0))
        for kind in range(3):
            for extra in range(GROUP - 1):
                put(room * kind + found[kind] + extra, 0, 0, 0.0)
            index_ref[at, 6 * room + kind] = (found[kind] + GROUP - 1) // GROUP
        index_ref[at, 6 * room + 3] = meta_ref[1]


def room_of(index_ref):
    return index_ref.shape[1] // 6


def first_kernel(first_ref, *refs):
    *piece_refs, out_ref = refs
    total = jnp.zeros(out_ref.shape, jnp.float32)
    for index, piece_ref in enumerate(piece_refs):
        total += exact_product(first_ref[index], piece_ref[...])
    out_ref[...] = total.astype(out_ref.dtype)


def add_slots(sum_ref, stored, dep_row, kind, index_ref, weight_ref, blocks_ref):
    room = room_of(index_ref)
    at = max(dep_row - 1, 0)

    def add_group(step, carry):
        total = sum_ref[...]
        for offset in range(GROUP):
            position = room * kind + GROUP * step + offset
            part = product(
                blocks_ref[at, index_ref[at, position]],
                stored[index_ref[at, 3 * room + position]],
            )
            total += weight_ref[at, position] * part
        sum_ref[...] = total
        return carry

    lax.fori_loop(0, index_ref[at, 6 * room + kind], add_group, 0)


def early_kernel(level, index_ref, weight_ref, blocks_ref, right_ref, *refs):
    *piece_refs, sum_ref, stored_ref = refs
    start = 0
    for piece_ref in piece_refs:
        stored_ref[pl.ds(start, piece_ref.shape[0])] = piece_ref[...]
        start += piece_ref.shape[0]
    share = right_ref.shape[1]
    sum_ref[...] = jnp.zeros_like(sum_ref)
    start = pl.multiple_of(index_ref[0, 6 * room_of(index_ref) + 3] * share, share)
    sum_ref[pl.ds(start, share), :] = right_ref[level]
    add_slots(sum_ref, stored_ref, level - 1, 2, index_ref, weight_ref, blocks_ref)


def middle_kernel(level, index_ref, weight_ref, blocks_ref, before_ref, mine_ref, sum_ref):
    sum_ref[...] = before_ref[...]
    add_slots(sum_ref, mine_ref, level - 1, 1, index_ref, weight_ref, blocks_ref)


def last_kernel(level, index_ref, weight_ref, blocks_ref, before_ref, theirs_ref, *refs):
    *diag_refs, own_ref, one_ref, two_ref, across_ref, sum_ref = refs
    sum_ref[...] = before_ref[...]
    add_slots(sum_ref, theirs_ref, level - 1, 0, index_ref, weight_ref, blocks_ref)
    blocks = jnp.concatenate([ref[...] for ref in diag_refs], axis=0)
    total = exact_product(blocks, sum_ref[...])
    share = own_ref.shape[0]
    for index, ref in enumerate((own_ref, one_ref, two_ref, across_ref)):
        ref[...] = total[index * share : (index + 1) * share].astype(ref.dtype)


def per_device(factor_blocks, block_scales, dep_column, dep_count, diag_inverse, right_side):
    level_count, share, block_rows = diag_inverse.shape
    slots = factor_blocks.shape[1]
    width = right_side.shape[2]
    rows, cols = lax.axis_size("row"), lax.axis_size("col")
    shard = lax.axis_index("row").astype(jnp.int32)
    col = lax.axis_index("col").astype(jnp.int32)
    even = shard % 2 == 0
    one = jnp.where(even, col ^ 1, cols - 1 - col)
    two = jnp.where(even, cols - 1 - col, col ^ 1)
    meta = jnp.stack([shard, col, one, two, (col + 2) % cols])
    bf16, f32 = jnp.bfloat16, jnp.float32
    shape = jax.ShapeDtypeStruct
    room = slots + GROUP - 1
    soon = 2
    late = level_count - 1 - soon
    wide = shape((block_rows, width), f32)
    piece = shape((share, width), bf16)

    def call(body, out_shape, in_specs, out_specs, operands, limit, scratch=(), flops=2**27, name=None):
        return pl.pallas_call(
            body,
            out_shape=out_shape,
            in_specs=in_specs,
            out_specs=out_specs,
            scratch_shapes=list(scratch),
            cost_estimate=pl.CostEstimate(flops=flops, bytes_accessed=2 * MIB, transcendentals=0),
            compiler_params=pltpu.CompilerParams(vmem_limit_bytes=limit),
            name=name,
        )(*operands)

    def along_col(value, which):
        return lax.ppermute(value, ("col", "row"), col_moves(cols, rows, which))

    def swap(value):
        return lax.ppermute(value, "row", swap_moves(rows))

    def after(value, *others):
        return lax.optimization_barrier((value, *others))[0]

    own = right_side[0]
    arrived = [along_col(own, which) for which in (2, 0, 1)]
    diag_later = after(diag_inverse, own)
    soon_diag, start_diag = diag_later[1 : 1 + soon], diag_later[0]
    soon_one = along_col(soon_diag, 0)

    def list_slots(rows, meta):
        return call(
            functools.partial(table_kernel, level_count, rows),
            [shape((len(rows), 6 * room + 4), jnp.int32), shape((len(rows), 3 * room), f32)],
            [SMEM] * 4,
            [SMEM] * 2,
            (meta, dep_column, dep_count, block_scales),
            TABLE_LIMIT,
            name="table",
        )

    first = call(
        order_kernel,
        shape((4, share, share), bf16),
        [SMEM, VMEM],
        VMEM,
        (after(meta, own), start_diag),
        2 * MIB,
        name="order",
    )
    index, weight = list_slots((0,), after(meta, own))
    blocks = call(
        soon_fill_kernel,
        shape((1, *factor_blocks.shape[1:]), bf16),
        [HBM],
        VMEM,
        (after(factor_blocks, own),),
        SOON_LIMIT,
        [pltpu.SemaphoreType.DMA((1,))],
        name="soon_fill",
    )
    opposite, by_one, by_two = arrived
    opposite, by_one, by_two, first, blocks, soon_one, index = lax.optimization_barrier(
        (opposite, by_one, by_two, first, blocks, soon_one, index)
    )
    solved = call(
        first_kernel,
        piece,
        [VMEM] * 5,
        VMEM,
        (first, own, by_one, by_two, opposite),
        4 * MIB,
        name="first_solve",
    )
    outputs = [solved]
    pieces = []
    diags = {}
    for level in range(1, level_count):
        other = swap(solved)
        pair = jnp.where(even, jnp.stack([solved, other]), jnp.stack([other, solved]))
        far = lax.ppermute(pair, "row", row_moves(rows, 2))
        near = lax.ppermute(pair, "row", row_moves(rows, 1))
        far_first = far
        stored = after([pair, *(x for three in pieces for x in three)], pair)
        if level == 2:
            index, weight = list_slots(tuple(range(1, level_count - 1)), after(meta, pair))
            blocks = late_blocks
        tables = (index, weight, blocks)
        table_specs = [SMEM] * 2 + [VMEM]
        early = call(
            functools.partial(early_kernel, level),
            wide,
            table_specs + [VMEM] * (1 + len(stored)),
            VMEM,
            (*tables, right_side, *stored),
            20 * MIB,
            [pltpu.VMEM((2 + 10 * (level - 1), share, width), bf16)],
            name="early_slots",
        )
        ready = [near, far, early]
        if level == 1:
            soon_two = along_col(after(jnp.stack([soon_diag, soon_one]), early), 1)
            for at in range(soon):
                diags[1 + at] = (soon_diag[at], soon_one[at], soon_two[0, at], soon_two[1, at])
            fill = call(
                late_fill_kernel,
                [
                    shape((level_count - 2, *factor_blocks.shape[1:]), bf16),
                    shape((late, share, block_rows), bf16),
                ],
                [HBM, HBM],
                [VMEM, VMEM],
                (after(factor_blocks, early), diag_inverse),
                LATE_LIMIT,
                [pltpu.SemaphoreType.DMA((2,))],
                name="late_fill",
            )
            ready += fill
            near, far, early, late_blocks, late_diag = lax.optimization_barrier(ready)
            half_way = along_col(after(fill[1][0], far_first), 1)
            which = 0
        else:
            near, far, early = lax.optimization_barrier(ready)
            ahead = level + 1
            if ahead < level_count:
                mine_diag = late_diag[ahead - 1 - soon]
                sent = [mine_diag, half_way]
                if ahead + 1 < level_count:
                    sent.append(late_diag[ahead - soon])
                got = along_col(after(jnp.stack(sent), far_first), which)
                by = (got[0], half_way) if which == 0 else (half_way, got[0])
                diags[ahead] = (mine_diag, *by, got[1])
                half_way = got[2] if ahead + 1 < level_count else None
                which = 1 - which
        mine = jnp.concatenate([near, far], axis=0)
        theirs = swap(mine)
        middle = call(
            functools.partial(middle_kernel, level),
            wide,
            table_specs + [VMEM] * 2,
            VMEM,
            (*tables, early, mine),
            20 * MIB,
            name="middle_slots",
        )
        theirs, middle = lax.optimization_barrier((theirs, middle))
        pieces.append((pair, mine, theirs))
        own, *parts = call(
            functools.partial(last_kernel, level),
            [shape((share, width), f32)] + [piece] * 3,
            table_specs + [VMEM] * 6,
            [VMEM] * 4,
            (*tables, middle, theirs, *diags[level]),
            20 * MIB,
            [pltpu.VMEM((block_rows, width), f32)],
            name="last_slots",
        )
        total = own
        for which_part in (2, 0, 1):
            total = total + along_col(parts[which_part], which_part).astype(f32)
        solved = total.astype(bf16)
        outputs.append(solved)
    return jnp.stack(outputs, axis=0)


def solution(mesh):
    in_specs = (
        P("row", None, None, "col"),
        P("row", None),
        P("row", None),
        P("row"),
        P("row", "col", None),
        P("row", "col", None),
    )
    return jax.shard_map(
        per_device, mesh=mesh, in_specs=in_specs, out_specs=P("row", "col", None), check_vma=False
    )
```

```python
import functools

import jax
import jax.numpy as jnp
from jax import lax
from jax.experimental import pallas as pl
from jax.experimental.pallas import tpu as pltpu
from jax.sharding import PartitionSpec as P

VMEM = pl.BlockSpec(memory_space=pltpu.VMEM)
SMEM = pl.BlockSpec(memory_space=pltpu.SMEM)
HBM = pl.BlockSpec(memory_space=pltpu.HBM)
MIB = 2**20
GROUP = 4
NEAR = 8
TABLE_LIMIT = 2 * MIB
SOON_LIMIT = 48 * MIB
LATE_LIMIT = 40 * MIB


def row_moves(count, delta):
    pairs = []
    for target in range(count):
        step = 2 * delta if target % 2 == 0 else -2 * delta
        pairs.append(((target + step) % count, target))
    return pairs


def swap_moves(count):
    return [(source, source ^ 1) for source in range(count)]


def partners(cols, col, odd):
    one, two = (col ^ 1, cols - 1 - col) if odd == 0 else (cols - 1 - col, col ^ 1)
    return one, two, (col + 2) % cols


def col_moves(cols, rows, which):
    return [
        (col * rows + row, partners(cols, col, row % 2)[which] * rows + row)
        for col in range(cols)
        for row in range(rows)
    ]


def split(value):
    high = value.astype(jnp.bfloat16)
    return high, (value - high.astype(jnp.float32)).astype(jnp.bfloat16)


def product(left, right):
    return jnp.dot(left, right, preferred_element_type=jnp.float32)


def exact_product(left, right):
    high, low = split(right)
    return product(left, high) + product(left, low)


def run_copies(copies):
    for copy in copies:
        copy.start()
    for copy in copies:
        copy.wait()


def fill_kernel(source_ref, start, out_ref, sem):
    run_copies([pltpu.make_async_copy(source_ref.at[pl.ds(start, out_ref.shape[0])], out_ref, sem)])


def soon_fill_kernel(factor_ref, out_ref, sems):
    fill_kernel(factor_ref, 0, out_ref, sems.at[0])


def late_fill_kernel(factor_ref, out_ref, sems):
    fill_kernel(factor_ref, 1, out_ref, sems.at[0])


def order_kernel(meta_ref, start_ref, first_ref):
    share = first_ref.shape[1]
    for index in range(4):
        start = pl.multiple_of(meta_ref[1 + index] * share, share)
        first_ref[index] = start_ref[:, pl.ds(start, share)]


def table_kernel(
    level_count, dep_rows, meta_ref, column_ref, count_ref, scale_ref, index_ref, weight_ref
):
    own_chip = meta_ref[0] // 2
    turn = 1 - 2 * (meta_ref[0] % 2)
    room = weight_ref.shape[1]
    inverse = (2**16 + level_count - 1) // level_count
    for at, dep_row in enumerate(dep_rows):
        for position in range(NEAR):
            index_ref[at, position] = 0
            weight_ref[at, position] = 0.0

        def put(position, slot, place, scale):
            index_ref[at, position] = slot
            index_ref[at, room + position] = place
            weight_ref[at, position] = -scale

        def collect(slot, found):
            column = column_ref[dep_row, slot]
            shard = lax.shift_right_logical(column * inverse, 16)
            from_level = column - shard * level_count
            forward = (lax.shift_right_logical(shard, 1) - own_chip) * turn
            parity = lax.bitwise_and(shard, 1)
            rest = (from_level != dep_row) | (forward == 0)
            piece = parity + jnp.where(forward == 0, 0, 2 * jnp.abs(forward) - 2)
            start = jnp.where(forward == 0, 2, jnp.where(forward > 0, 4, 8))
            place = jnp.where(from_level != dep_row, 10 * from_level + start, 0) + piece
            position = jnp.where(rest, NEAR + found, jnp.where(forward > 0, 4, 0) + piece)
            put(position, slot, place, scale_ref[dep_row, slot])
            return found + rest.astype(jnp.int32)

        found = lax.fori_loop(0, count_ref[dep_row], collect, 0)
        for extra in range(GROUP - 1):
            put(NEAR + found + extra, 0, 0, 0.0)
        index_ref[at, 2 * room] = (found + GROUP - 1) // GROUP
        index_ref[at, 2 * room + 1] = meta_ref[1]


def first_kernel(first_ref, *refs):
    own_ref, *piece_refs, out_ref = refs
    total = exact_product(first_ref[0], own_ref[...])
    for index, piece_ref in enumerate(piece_refs):
        total += product(first_ref[1 + index], piece_ref[...])
    out_ref[...] = total.astype(out_ref.dtype)


def early_kernel(level, row, index_ref, weight_ref, blocks_ref, right_ref, *refs):
    *piece_refs, sum_ref, near_ref, near_weight_ref, stored_ref = refs
    at = max(level - 2, 0)
    room = weight_ref.shape[1]
    start = 0
    for piece_ref in piece_refs:
        stored_ref[pl.ds(start, piece_ref.shape[0])] = piece_ref[...]
        start += piece_ref.shape[0]
    share = right_ref.shape[1]
    sum_ref[...] = jnp.zeros_like(sum_ref)
    start = pl.multiple_of(index_ref[row, 2 * room + 1] * share, share)
    sum_ref[pl.ds(start, share), :] = right_ref[level]

    def add_group(step, carry):
        total = sum_ref[...]
        for offset in range(GROUP):
            position = NEAR + GROUP * step + offset
            part = product(
                blocks_ref[at, index_ref[row, position]],
                stored_ref[index_ref[row, room + position]],
            )
            total += weight_ref[row, position] * part
        sum_ref[...] = total
        return carry

    lax.fori_loop(0, index_ref[row, 2 * room], add_group, 0)
    for position in range(NEAR):
        near_ref[position] = blocks_ref[at, index_ref[row, position]]
        near_weight_ref[position] = jnp.full(near_weight_ref.shape[1:], weight_ref[row, position])


def with_pieces(total, first, near_ref, near_weight_ref, pieces_ref):
    for index in range(pieces_ref.shape[0]):
        part = product(near_ref[first + index], pieces_ref[index])
        total += near_weight_ref[first + index] * part
    return total


def middle_kernel(near_ref, near_weight_ref, before_ref, mine_ref, sum_ref):
    sum_ref[...] = with_pieces(before_ref[...], 4, near_ref, near_weight_ref, mine_ref)


def last_kernel(near_ref, near_weight_ref, before_ref, theirs_ref, *refs):
    *diag_refs, own_ref, one_ref, two_ref, across_ref = refs
    total = with_pieces(before_ref[...], 0, near_ref, near_weight_ref, theirs_ref)
    blocks = jnp.concatenate([ref[...] for ref in diag_refs], axis=0)
    total = exact_product(blocks, total)
    share = own_ref.shape[0]
    for index, ref in enumerate((own_ref, one_ref, two_ref, across_ref)):
        ref[...] = total[index * share : (index + 1) * share].astype(ref.dtype)


def per_device(factor_blocks, block_scales, dep_column, dep_count, diag_inverse, right_side):
    level_count, share, block_rows = diag_inverse.shape
    slots = factor_blocks.shape[1]
    width = right_side.shape[2]
    rows, cols = lax.axis_size("row"), lax.axis_size("col")
    shard = lax.axis_index("row").astype(jnp.int32)
    col = lax.axis_index("col").astype(jnp.int32)
    even = shard % 2 == 0
    one = jnp.where(even, col ^ 1, cols - 1 - col)
    two = jnp.where(even, cols - 1 - col, col ^ 1)
    meta = jnp.stack([shard, col, one, two, (col + 2) % cols])
    bf16, f32 = jnp.bfloat16, jnp.float32
    shape = jax.ShapeDtypeStruct
    room = NEAR + slots + GROUP - 1
    wide = shape((block_rows, width), f32)
    piece = shape((share, width), bf16)

    def call(body, out_shape, in_specs, out_specs, operands, limit, scratch=(), flops=2**27, name=None):
        return pl.pallas_call(
            body,
            out_shape=out_shape,
            in_specs=in_specs,
            out_specs=out_specs,
            scratch_shapes=list(scratch),
            cost_estimate=pl.CostEstimate(flops=flops, bytes_accessed=2 * MIB, transcendentals=0),
            compiler_params=pltpu.CompilerParams(vmem_limit_bytes=limit),
            name=name,
        )(*operands)

    def along_col(value, which):
        return lax.ppermute(value, ("col", "row"), col_moves(cols, rows, which))

    def swap(value):
        return lax.ppermute(value, "row", swap_moves(rows))

    def after(value, *others):
        return lax.optimization_barrier((value, *others))[0]

    own = right_side[0]
    own_rounded = own.astype(bf16)
    arrived = [along_col(own_rounded, which) for which in (2, 0, 1)]
    diag_later = after(diag_inverse, own_rounded)
    start_diag, *own_diags = [diag_later[at] for at in range(level_count)]
    half_way = along_col(own_diags[0], 0)

    def list_slots(dep_rows, meta):
        return call(
            functools.partial(table_kernel, level_count, dep_rows),
            [shape((len(dep_rows), 2 * room + 2), jnp.int32), shape((len(dep_rows), room), f32)],
            [SMEM] * 4,
            [SMEM] * 2,
            (meta, dep_column, dep_count, block_scales),
            TABLE_LIMIT,
            name="table",
        )

    first = call(
        order_kernel,
        shape((4, share, share), bf16),
        [SMEM, VMEM],
        VMEM,
        (after(meta, own_rounded), start_diag),
        2 * MIB,
        name="order",
    )
    opposite, by_one, by_two = arrived
    opposite, by_one, by_two, first = lax.optimization_barrier((opposite, by_one, by_two, first))
    solved = call(
        first_kernel,
        piece,
        [VMEM] * 5,
        VMEM,
        (first, own, by_one, by_two, opposite),
        4 * MIB,
        name="first_solve",
    )
    outputs = [solved]
    pieces = []
    diags = {}
    late = level_count - 3
    for level in range(1, level_count):
        other = swap(solved)
        if level == 1:
            sent = [own_diags[0], half_way, own_diags[1]]
            got = along_col(after(jnp.stack(sent), solved), 1)
            diags[1] = (own_diags[0], half_way, got[0], got[1])
            half_way = got[2]
        elif level == 2:
            sent = [own_diags[1], half_way, *own_diags[2:]]
            got = along_col(after(jnp.stack(sent), solved), 0)
            diags[2] = (own_diags[1], got[0], half_way, got[1])
            by_one_diags = got[2:]
        elif level == 3:
            sent = [*own_diags[2:], *(by_one_diags[at] for at in range(late))]
            got = along_col(after(jnp.stack(sent), solved), 1)
            for at in range(late):
                diags[3 + at] = (own_diags[2 + at], by_one_diags[at], got[at], got[late + at])
        pair = jnp.where(even, jnp.stack([solved, other]), jnp.stack([other, solved]))
        far = lax.ppermute(pair, "row", row_moves(rows, 2))
        near = lax.ppermute(pair, "row", row_moves(rows, 1))
        stored = after([pair, *(x for three in pieces for x in three)], pair)
        if level == 1:
            index, weight = list_slots((0, 1), after(meta, pair))
            blocks = call(
                soon_fill_kernel,
                shape((1, *factor_blocks.shape[1:]), bf16),
                [HBM],
                VMEM,
                (after(factor_blocks, pair),),
                SOON_LIMIT,
                [pltpu.SemaphoreType.DMA((1,))],
                name="soon_fill",
            )
        early, near_blocks, near_weight = call(
            functools.partial(early_kernel, level, 1 if level == 2 else 0),
            [
                wide,
                shape((NEAR, *factor_blocks.shape[2:]), bf16),
                shape((NEAR, 1, width), f32),
            ],
            [SMEM] * 2 + [VMEM] * (2 + len(stored)),
            [VMEM] * 3,
            (index, weight, blocks, right_side, *stored),
            20 * MIB,
            [pltpu.VMEM((2 + 10 * (level - 1), share, width), bf16)],
            name="early_slots",
        )
        near, far, early = lax.optimization_barrier((near, far, early))
        mine = jnp.concatenate([near, far], axis=0)
        theirs = swap(mine)
        middle = call(
            middle_kernel,
            wide,
            [VMEM] * 4,
            VMEM,
            (near_blocks, near_weight, early, mine),
            8 * MIB,
            name="middle_slots",
        )
        theirs, middle = lax.optimization_barrier((theirs, middle))
        pieces.append((pair, mine, theirs))
        own, *parts = call(
            last_kernel,
            [shape((share, width), f32)] + [piece] * 3,
            [VMEM] * 8,
            [VMEM] * 4,
            (near_blocks, near_weight, middle, theirs, *diags[level]),
            8 * MIB,
            name="last_slots",
        )
        arrived = [along_col(parts[which_part], which_part) for which_part in (2, 0, 1)]
        if level == 1:
            blocks = call(
                late_fill_kernel,
                shape((level_count - 2, *factor_blocks.shape[1:]), bf16),
                [HBM],
                VMEM,
                (after(factor_blocks, parts[0]),),
                LATE_LIMIT,
                [pltpu.SemaphoreType.DMA((1,))],
                name="late_fill",
            )
            *arrived, blocks = lax.optimization_barrier((*arrived, blocks))
        elif level + 1 < level_count:
            index, weight = list_slots((level,), after(meta, parts[0]))
            *arrived, index = lax.optimization_barrier((*arrived, index))
        total = own
        for part in arrived:
            total = total + part.astype(f32)
        solved = total.astype(bf16)
        outputs.append(solved)
    return jnp.stack(outputs, axis=0)


def solution(mesh):
    in_specs = (
        P("row", None, None, "col"),
        P("row", None),
        P("row", None),
        P("row"),
        P("row", "col", None),
        P("row", "col", None),
    )
    return jax.shard_map(
        per_device, mesh=mesh, in_specs=in_specs, out_specs=P("row", "col", None), check_vma=False
    )
```

```python
import functools

import jax
import jax.numpy as jnp
from jax import lax
from jax.experimental import pallas as pl
from jax.experimental.pallas import tpu as pltpu
from jax.sharding import PartitionSpec as P

VMEM = pl.BlockSpec(memory_space=pltpu.VMEM)
SMEM = pl.BlockSpec(memory_space=pltpu.SMEM)
HBM = pl.BlockSpec(memory_space=pltpu.HBM)
MIB = 2**20
GROUP = 4
NEAR = 8
TABLE_LIMIT = 2 * MIB
SOON_LIMIT = 48 * MIB
LATE_LIMIT = 40 * MIB


def row_moves(count, delta):
    pairs = []
    for target in range(count):
        step = 2 * delta if target % 2 == 0 else -2 * delta
        pairs.append(((target + step) % count, target))
    return pairs


def swap_moves(count):
    return [(source, source ^ 1) for source in range(count)]


def partners(cols, col, odd):
    one, two = (col ^ 1, cols - 1 - col) if odd == 0 else (cols - 1 - col, col ^ 1)
    return one, two, (col + 2) % cols


def col_moves(cols, rows, which):
    return [
        (col * rows + row, partners(cols, col, row % 2)[which] * rows + row)
        for col in range(cols)
        for row in range(rows)
    ]


def split(value):
    high = value.astype(jnp.bfloat16)
    return high, (value - high.astype(jnp.float32)).astype(jnp.bfloat16)


def product(left, right):
    return jnp.dot(left, right, preferred_element_type=jnp.float32)


def exact_product(left, right):
    high, low = split(right)
    return product(left, high) + product(left, low)


def run_copies(copies):
    for copy in copies:
        copy.start()
    for copy in copies:
        copy.wait()


def fill_kernel(source_ref, start, out_ref, sem):
    run_copies([pltpu.make_async_copy(source_ref.at[pl.ds(start, out_ref.shape[0])], out_ref, sem)])


def soon_fill_kernel(factor_ref, out_ref, sems):
    fill_kernel(factor_ref, 0, out_ref, sems.at[0])


def late_fill_kernel(factor_ref, out_ref, sems):
    fill_kernel(factor_ref, 1, out_ref, sems.at[0])


def order_kernel(meta_ref, start_ref, first_ref):
    share = first_ref.shape[1]
    for index in range(4):
        start = pl.multiple_of(meta_ref[1 + index] * share, share)
        first_ref[index] = start_ref[:, pl.ds(start, share)]


def table_kernel(
    level_count, dep_rows, meta_ref, column_ref, count_ref, scale_ref, index_ref, weight_ref
):
    own_chip = meta_ref[0] // 2
    turn = 1 - 2 * (meta_ref[0] % 2)
    room = weight_ref.shape[1]
    inverse = (2**16 + level_count - 1) // level_count
    for at, dep_row in enumerate(dep_rows):
        for position in range(NEAR):
            index_ref[at, position] = 0
            weight_ref[at, position] = 0.0

        def put(position, slot, place, scale):
            index_ref[at, position] = slot
            index_ref[at, room + position] = place
            weight_ref[at, position] = -scale

        def collect(slot, found):
            column = column_ref[dep_row, slot]
            shard = lax.shift_right_logical(column * inverse, 16)
            from_level = column - shard * level_count
            forward = (lax.shift_right_logical(shard, 1) - own_chip) * turn
            parity = lax.bitwise_and(shard, 1)
            rest = (from_level != dep_row) | (forward == 0)
            piece = parity + jnp.where(forward == 0, 0, 2 * jnp.abs(forward) - 2)
            start = jnp.where(forward == 0, 2, jnp.where(forward > 0, 4, 8))
            place = jnp.where(from_level != dep_row, 10 * from_level + start, 0) + piece
            position = jnp.where(rest, NEAR + found, jnp.where(forward > 0, 4, 0) + piece)
            put(position, slot, place, scale_ref[dep_row, slot])
            return found + rest.astype(jnp.int32)

        found = lax.fori_loop(0, count_ref[dep_row], collect, 0)
        for extra in range(GROUP - 1):
            put(NEAR + found + extra, 0, 0, 0.0)
        index_ref[at, 2 * room] = (found + GROUP - 1) // GROUP
        index_ref[at, 2 * room + 1] = meta_ref[1]


def first_kernel(first_ref, *refs):
    own_ref, *piece_refs, out_ref = refs
    total = exact_product(first_ref[0], own_ref[...])
    for index, piece_ref in enumerate(piece_refs):
        total += product(first_ref[1 + index], piece_ref[...])
    out_ref[...] = total.astype(out_ref.dtype)


def early_kernel(level, row, index_ref, weight_ref, blocks_ref, right_ref, *refs):
    *piece_refs, sum_ref, near_ref, near_weight_ref, stored_ref = refs
    at = max(level - 2, 0)
    room = weight_ref.shape[1]
    start = 0
    for piece_ref in piece_refs:
        stored_ref[pl.ds(start, piece_ref.shape[0])] = piece_ref[...]
        start += piece_ref.shape[0]
    share = right_ref.shape[1]
    sum_ref[...] = jnp.zeros_like(sum_ref)
    start = pl.multiple_of(index_ref[row, 2 * room + 1] * share, share)
    sum_ref[pl.ds(start, share), :] = right_ref[level]

    def add_group(step, carry):
        total = sum_ref[...]
        for offset in range(GROUP):
            position = NEAR + GROUP * step + offset
            part = product(
                blocks_ref[at, index_ref[row, position]],
                stored_ref[index_ref[row, room + position]],
            )
            total += weight_ref[row, position] * part
        sum_ref[...] = total
        return carry

    lax.fori_loop(0, index_ref[row, 2 * room], add_group, 0)
    for position in range(NEAR):
        near_ref[position] = blocks_ref[at, index_ref[row, position]]
        near_weight_ref[position] = jnp.full(near_weight_ref.shape[1:], weight_ref[row, position])


def with_pieces(total, first, near_ref, near_weight_ref, pieces_ref):
    for index in range(pieces_ref.shape[0]):
        part = product(near_ref[first + index], pieces_ref[index])
        total += near_weight_ref[first + index] * part
    return total


def middle_kernel(near_ref, near_weight_ref, before_ref, mine_ref, sum_ref):
    sum_ref[...] = with_pieces(before_ref[...], 4, near_ref, near_weight_ref, mine_ref)


def last_kernel(near_ref, near_weight_ref, before_ref, theirs_ref, *refs):
    *diag_refs, own_ref, one_ref, two_ref, across_ref = refs
    total = with_pieces(before_ref[...], 0, near_ref, near_weight_ref, theirs_ref)
    blocks = jnp.concatenate([ref[...] for ref in diag_refs], axis=0)
    total = exact_product(blocks, total)
    share = own_ref.shape[0]
    for index, ref in enumerate((own_ref, one_ref, two_ref, across_ref)):
        ref[...] = total[index * share : (index + 1) * share].astype(ref.dtype)


def per_device(factor_blocks, block_scales, dep_column, dep_count, diag_inverse, right_side):
    level_count, share, block_rows = diag_inverse.shape
    slots = factor_blocks.shape[1]
    width = right_side.shape[2]
    rows, cols = lax.axis_size("row"), lax.axis_size("col")
    shard = lax.axis_index("row").astype(jnp.int32)
    col = lax.axis_index("col").astype(jnp.int32)
    even = shard % 2 == 0
    one = jnp.where(even, col ^ 1, cols - 1 - col)
    two = jnp.where(even, cols - 1 - col, col ^ 1)
    meta = jnp.stack([shard, col, one, two, (col + 2) % cols])
    bf16, f32 = jnp.bfloat16, jnp.float32
    shape = jax.ShapeDtypeStruct
    room = NEAR + slots + GROUP - 1
    wide = shape((block_rows, width), f32)
    piece = shape((share, width), bf16)

    def call(body, out_shape, in_specs, out_specs, operands, limit, scratch=(), flops=2**27, name=None):
        return pl.pallas_call(
            body,
            out_shape=out_shape,
            in_specs=in_specs,
            out_specs=out_specs,
            scratch_shapes=list(scratch),
            cost_estimate=pl.CostEstimate(flops=flops, bytes_accessed=2 * MIB, transcendentals=0),
            compiler_params=pltpu.CompilerParams(vmem_limit_bytes=limit),
            name=name,
        )(*operands)

    def along_col(value, which):
        return lax.ppermute(value, ("col", "row"), col_moves(cols, rows, which))

    def swap(value):
        return lax.ppermute(value, "row", swap_moves(rows))

    def after(value, *others):
        return lax.optimization_barrier((value, *others))[0]

    own = right_side[0]
    own_rounded = own.astype(bf16)
    arrived = [along_col(own_rounded, which) for which in (2, 0, 1)]
    diag_later = after(diag_inverse, own_rounded)
    start_diag, *own_diags = [diag_later[at] for at in range(level_count)]
    half_way = along_col(jnp.stack(own_diags[:2]), 0)

    def list_slots(dep_rows, meta):
        return call(
            functools.partial(table_kernel, level_count, dep_rows),
            [shape((len(dep_rows), 2 * room + 2), jnp.int32), shape((len(dep_rows), room), f32)],
            [SMEM] * 4,
            [SMEM] * 2,
            (meta, dep_column, dep_count, block_scales),
            TABLE_LIMIT,
            name="table",
        )

    first = call(
        order_kernel,
        shape((4, share, share), bf16),
        [SMEM, VMEM],
        VMEM,
        (after(meta, own_rounded), start_diag),
        2 * MIB,
        name="order",
    )
    opposite, by_one, by_two = arrived
    opposite, by_one, by_two, first = lax.optimization_barrier((opposite, by_one, by_two, first))
    solved = call(
        first_kernel,
        piece,
        [VMEM] * 5,
        VMEM,
        (first, own, by_one, by_two, opposite),
        4 * MIB,
        name="first_solve",
    )
    outputs = [solved]
    pieces = []
    diags = {}
    late = level_count - 3
    for level in range(1, level_count):
        other = swap(solved)
        if level == 2:
            sent = [own_diags[1], half_way[1], *own_diags[2:]]
            got = along_col(after(jnp.stack(sent), solved), 1)
            diags[2] = (own_diags[1], half_way[1], got[0], got[1])
            by_two_diags = got[2:]
        elif level == 3:
            sent = [*own_diags[2:], *(by_two_diags[at] for at in range(late))]
            got = along_col(after(jnp.stack(sent), solved), 0)
            for at in range(late):
                diags[3 + at] = (own_diags[2 + at], got[at], by_two_diags[at], got[late + at])
        pair = jnp.where(even, jnp.stack([solved, other]), jnp.stack([other, solved]))
        far = lax.ppermute(pair, "row", row_moves(rows, 2))
        near = lax.ppermute(pair, "row", row_moves(rows, 1))
        stored = after([pair, *(x for three in pieces for x in three)], pair)
        if level == 1:
            blocks = call(
                soon_fill_kernel,
                shape((1, *factor_blocks.shape[1:]), bf16),
                [HBM],
                VMEM,
                (after(factor_blocks, pair),),
                SOON_LIMIT,
                [pltpu.SemaphoreType.DMA((1,))],
                name="soon_fill",
            )
            got = along_col(after(jnp.stack([own_diags[0], half_way[0]]), blocks), 1)
            diags[1] = (own_diags[0], half_way[0], got[0], got[1])
            index, weight = list_slots((0, 1), after(meta, blocks))
        early, near_blocks, near_weight = call(
            functools.partial(early_kernel, level, 1 if level == 2 else 0),
            [
                wide,
                shape((NEAR, *factor_blocks.shape[2:]), bf16),
                shape((NEAR, 1, width), f32),
            ],
            [SMEM] * 2 + [VMEM] * (2 + len(stored)),
            [VMEM] * 3,
            (index, weight, blocks, right_side, *stored),
            20 * MIB,
            [pltpu.VMEM((2 + 10 * (level - 1), share, width), bf16)],
            name="early_slots",
        )
        near, far, early = lax.optimization_barrier((near, far, early))
        mine = jnp.concatenate([near, far], axis=0)
        theirs = swap(mine)
        middle = call(
            middle_kernel,
            wide,
            [VMEM] * 4,
            VMEM,
            (near_blocks, near_weight, early, mine),
            8 * MIB,
            name="middle_slots",
        )
        theirs, middle = lax.optimization_barrier((theirs, middle))
        pieces.append((pair, mine, theirs))
        own, *parts = call(
            last_kernel,
            [shape((share, width), f32)] + [piece] * 3,
            [VMEM] * 8,
            [VMEM] * 4,
            (near_blocks, near_weight, middle, theirs, *diags[level]),
            8 * MIB,
            name="last_slots",
        )
        arrived = [along_col(parts[which_part], which_part) for which_part in (2, 0, 1)]
        if level == 1:
            blocks = call(
                late_fill_kernel,
                shape((level_count - 2, *factor_blocks.shape[1:]), bf16),
                [HBM],
                VMEM,
                (after(factor_blocks, parts[0]),),
                LATE_LIMIT,
                [pltpu.SemaphoreType.DMA((1,))],
                name="late_fill",
            )
            *arrived, blocks = lax.optimization_barrier((*arrived, blocks))
        elif level + 1 < level_count:
            index, weight = list_slots((level,), after(meta, parts[0]))
            *arrived, index = lax.optimization_barrier((*arrived, index))
        total = own
        for part in arrived:
            total = total + part.astype(f32)
        solved = total.astype(bf16)
        outputs.append(solved)
    return jnp.stack(outputs, axis=0)


def solution(mesh):
    in_specs = (
        P("row", None, None, "col"),
        P("row", None),
        P("row", None),
        P("row"),
        P("row", "col", None),
        P("row", "col", None),
    )
    return jax.shard_map(
        per_device, mesh=mesh, in_specs=in_specs, out_specs=P("row", "col", None), check_vma=False
    )
```
